512 devices in a mesh: dp: 32 (over x, y, core), tensor: 16 (over z).
Axes of the slice: x: 4, y: 4, z: 16, core: 2. Of those that a mesh axis runs over, the one named last changes fastest.
Arguments:
- tokens: bfloat16 [2048, 16384], P('dp', 'tensor'), parts along dimension 0, may hold values from -6 to 6
- gate_up_base: bfloat16 [2048, 2, 53248], P('dp', None, 'tensor'), parts along dimension 0, may hold values from -6 to 6
- shrink_gate_up: bfloat16 [64, 2, 16384, 64], P('dp', None, 'tensor'), parts along dimension 0, may hold values from -0.046875 to 0.046875
- expand_gate_up: bfloat16 [64, 2, 64, 53248], P('dp', None, None, 'tensor'), parts along dimension 0, may hold values from -0.75 to 0.75
- shrink_down: bfloat16 [64, 53248, 64], P('dp', 'tensor'), parts along dimension 0, may hold values from -0.02734375 to 0.02734375
- expand_down: bfloat16 [64, 64, 16384], P('dp', None, 'tensor'), parts along dimension 0, may hold values from -0.75 to 0.75
- token_slot: int32 [2048], P('dp'), parts along dimension 0, may hold values from 0 to 1, never falling along the last dimension, each value on 1 to 48 neighbouring positions
Outputs:
- hidden: bfloat16 [2048, 53248], P('dp', 'tensor'), parts along dimension 0
- down_delta: bfloat16 [2048, 16384], P('dp', 'tensor'), parts along dimension 0
The draws below stay inside these ranges and needn't reach their ends.
There are 32 independent parts, one for each index of `dp`. The reference program is written for one: setup_inputs(seed, part) draws one part's arguments, and reference() takes and returns one part's arrays. A program takes and returns all parts, laid end to end along the dimension named above; each array names one. Nothing has to cross between parts.
Inputs may be any that keep to these rules, and one draw needn't show every extreme that they name: `token_slot`: slots never fall along the tokens; each of the 2 slots holds 1 to 48 tokens.
All inputs are finite; a program needn't handle non-finite values.
Results may differ from the reference program's by a relative error of at most 0.017.
Values may be sent and summed in bfloat16 or wider, within the bound.
A program may use at most 64 MiB of HBM per device.

```python
import math
import jax
import jax.numpy as jnp
import numpy as np

D = 16384
FF = 53248
RANK = 64
SLOTS = 2
TOK = 64


def steps_of(own_key, shape, split, least, top_value):
    def one(dim, parts):
        draws = jax.random.uniform(jax.random.fold_in(jax.random.fold_in(own_key, 6), dim), (parts,), jnp.float32, least / len(split), top_value / len(split))
        return jnp.repeat(jnp.exp(draws), shape[dim] // parts).reshape((-1,) + (1,) * (len(shape) - dim - 1))

    gain = one(*split[0])
    for cut in split[1:]:
        gain = gain * one(*cut)
    return gain


def profile(count, total, reach, slope):
    weights = [(1 << 20) // math.isqrt(rank ** slope) + 1 for rank in range(2, count + 1)]
    rest, counts = total - reach - (count - 1), [1] * (count - 1)
    while rest > 0:
        movable = [i for i in range(count - 1) if counts[i] < reach]
        mass, budget = sum([weights[i] for i in movable]), rest
        for i in movable:
            more = min(reach - counts[i], max(1, budget * weights[i] // mass), rest)
            counts[i] = counts[i] + more
            rest = rest - more
    return np.array([reach] + counts)


def uneven_parts(rng, amount, total, most, lean):
    if amount == 2:
        one = jax.random.randint(rng, (), max(1, total - most), min(most, total - 1) + 1)
        return jnp.stack([one, total - one])
    lengths = jnp.asarray(profile(amount, total, most, lean), jnp.int32)
    couples = (amount - 1) // 2
    donor, receiver = lengths[1:1 + 2 * couples:2], lengths[2:2 + 2 * couples:2]
    room = jnp.minimum(donor - 1, most - receiver)
    shifted = jax.random.randint(jax.random.fold_in(rng, 1), (couples,), 0, 1 << 20) % (room + 1)
    lengths = lengths.at[1:1 + 2 * couples:2].set(donor - shifted).at[2:2 + 2 * couples:2].set(receiver + shifted)
    return lengths[jax.random.permutation(jax.random.fold_in(rng, 2), amount)]


def normal_values(stream_key, extent, width, reach, shards=(), kind=jnp.bfloat16):
    drawn = jax.random.normal(stream_key, extent, jnp.float32) * width
    if len(shards) > 0:
        drawn = steps_of(stream_key, extent, shards, -0.22, 0.18) * drawn
    return jnp.clip(drawn, min=-reach, max=reach).astype(kind)


def setup_inputs(seed: int = 0, part: int = 0) -> dict:
    splits = jax.random.split(jax.random.key(seed), 8)
    part_keys = jax.random.split(jax.random.fold_in(splits[7], part), 8)
    tokens = normal_values(part_keys[0], (TOK, D), 1.0, 6.0, ((1, 16),))
    gate_up_base = normal_values(part_keys[1], (TOK, 2, FF), 1.0, 6.0, ((2, 16),))
    shrink_gate_up = normal_values(part_keys[2], (SLOTS, 2, D, RANK), D ** -0.5, 0.046875, ((2, 16),))
    expand_gate_up = normal_values(part_keys[3], (SLOTS, 2, RANK, FF), RANK ** -0.5, 0.75, ((3, 16),))
    shrink_down = normal_values(part_keys[4], (SLOTS, FF, RANK), FF ** -0.5, 0.02734375, ((1, 16),))
    expand_down = normal_values(part_keys[5], (SLOTS, RANK, D), RANK ** -0.5, 0.75, ((2, 16),))
    token_slot = jnp.searchsorted(jnp.cumsum(uneven_parts(part_keys[6], SLOTS, TOK, 3 * TOK // 4, 0)), jnp.arange(TOK), side="right").astype(jnp.int32)
    return dict(tokens=tokens, gate_up_base=gate_up_base, shrink_gate_up=shrink_gate_up, expand_gate_up=expand_gate_up, shrink_down=shrink_down, expand_down=expand_down, token_slot=token_slot)


def reference(tokens, gate_up_base, shrink_gate_up, expand_gate_up, shrink_down, expand_down, token_slot):
    selector = (token_slot[:, None] == jnp.arange(SLOTS, dtype=jnp.int32)[None, :]).astype(jnp.float32)
    folded = jnp.einsum("td,agdr->tagr", tokens.astype(jnp.float32), shrink_gate_up.astype(jnp.float32))
    shrunk = jnp.sum(folded * selector[:, :, None, None], axis=1).astype(jnp.bfloat16)
    widened = jnp.einsum("tgr,agrf->tagf", shrunk.astype(jnp.float32), expand_gate_up.astype(jnp.float32))
    preact = gate_up_base.astype(jnp.float32) + jnp.sum(widened * selector[:, :, None, None], axis=1)
    hidden = (jax.nn.silu(preact[:, 0]) * preact[:, 1]).astype(jnp.bfloat16)
    narrowed = jnp.einsum("tf,afr->tar", hidden.astype(jnp.float32), shrink_down.astype(jnp.float32))
    reduced = jnp.sum(narrowed * selector[:, :, None], axis=1).astype(jnp.bfloat16)
    expanded = jnp.einsum("tr,ard->tad", reduced.astype(jnp.float32), expand_down.astype(jnp.float32))
    down_delta = jnp.sum(expanded * selector[:, :, None], axis=1).astype(jnp.bfloat16)
    return hidden, down_delta
```

```python
import functools

import jax
import jax.numpy as jnp
from jax import lax
from jax.experimental import pallas as pl
from jax.experimental.pallas import tpu as pltpu
from jax.sharding import PartitionSpec as P

MESH = pl.DeviceIdType.MESH
NT = (((1,), (1,)), ((), ()))


def nt_dot(a, b):
    return lax.dot_general(a, b, NT, preferred_element_type=jnp.float32)


def dot(a, b):
    return jnp.dot(a, b, preferred_element_type=jnp.float32)


def kernel(
    tokens_hbm, base_hbm, shrink_up_hbm, expand_up_hbm, shrink_down_hbm, expand_down_hbm, slot_hbm,
    hidden_out, down_out,
    tokens, base, shrink_up, expand_up, shrink_down, expand_down, slot,
    planar, hidden, down,
    part, land_a, mine, land_b, part_down, land_c,
    in_sem, out_sem, send_a, recv_a, send_b, recv_b, send_c, recv_c,
):
    me = lax.axis_index("tensor")
    dp = lax.axis_index("dp")
    n = 16
    cube, spot = me // 4, me % 4

    def load(i, src, dst):
        c = pltpu.make_async_copy(src, dst, in_sem.at[i])
        c.start()
        return c

    def peer(z):
        return dict(device_id=(dp, z), device_id_type=MESH)

    def arrived(landing, sem):
        fifteen = landing.at[pl.ds(0, n - 1)]
        pltpu.make_async_copy(fifteen, fifteen, sem).wait()

    barrier = pltpu.get_barrier_semaphore()
    far_first = [8, 7, 9, 6, 10, 5, 11, 4, 12, 3, 13, 2, 14, 1, 15]
    for off in far_first:
        pl.semaphore_signal(barrier, inc=1, **peer((me + off) % n))

    first = [load(0, tokens_hbm, tokens), load(1, shrink_up_hbm, shrink_up), load(2, slot_hbm, slot)]
    second = [load(3, base_hbm, base), load(4, expand_up_hbm, expand_up)]
    third = [load(5, shrink_down_hbm, shrink_down), load(6, expand_down_hbm, expand_down)]
    for c in first:
        c.wait()

    ones = jnp.sum(slot[...].astype(jnp.float32), axis=1, keepdims=True)
    row = lax.broadcasted_iota(jnp.int32, (64, 128), 0).astype(jnp.float32)
    second_slot = row >= 64.0 - ones
    lane_low = lax.broadcasted_iota(jnp.int32, (64, 128), 1) < 64
    keep = lane_low != second_slot

    both = nt_dot(tokens[...], shrink_up[...])
    part[...] = jnp.where(second_slot, both[:, 128:], both[:, :128])

    pl.semaphore_wait(barrier, n - 1)

    copies = []
    for off in (1, 2, 3):
        to = (spot + off) % 4
        c = pltpu.make_async_remote_copy(
            src_ref=part.at[pl.ds(pl.multiple_of(to * 16, 16), 16)],
            dst_ref=land_a.at[off - 1],
            send_sem=send_a.at[off - 1],
            recv_sem=recv_a.at[off - 1],
            **peer(cube * 4 + to),
        )
        c.start()
        copies.append(c)

    for c in second:
        c.wait()
    planar[0] = base[:, 0, :].astype(jnp.float32)
    planar[1] = base[:, 1, :].astype(jnp.float32)

    own = pl.ds(pl.multiple_of(spot * 16, 16), 16)
    total = part[own, :]
    for c in copies:
        c.wait_recv()
    for i in range(3):
        total += land_a[i]
    mine[...] = total.astype(jnp.bfloat16)

    copies_b = []
    for i, off in enumerate(far_first):
        c = pltpu.make_async_remote_copy(
            src_ref=mine,
            dst_ref=land_b.at[me],
            send_sem=send_b.at[i],
            recv_sem=recv_b,
            **peer((me + off) % n),
        )
        c.start()
        copies_b.append(c)
    land_b[me] = mine[...]
    for c in third:
        c.wait()
    arrived(land_b, recv_b)

    shrunk = land_b[pl.ds(0, 4)].astype(jnp.float32)
    for i in range(1, 4):
        shrunk += land_b[pl.ds(4 * i, 4)].astype(jnp.float32)
    shrunk = shrunk.reshape(64, 128)
    swapped = pltpu.roll(shrunk, 64, 1)
    lhs = [
        jnp.where(keep, jnp.where(lane_low, shrunk, swapped), 0.0).astype(jnp.bfloat16),
        jnp.where(keep, jnp.where(lane_low, swapped, shrunk), 0.0).astype(jnp.bfloat16),
    ]
    narrowed = jnp.zeros((64, 128), jnp.float32)
    for k in range(13):
        cols = pl.ds(k * 256, 256)
        gate = dot(lhs[0], jnp.concatenate([expand_up[0, 0, :, cols], expand_up[1, 0, :, cols]], axis=0))
        up = dot(lhs[1], jnp.concatenate([expand_up[0, 1, :, cols], expand_up[1, 1, :, cols]], axis=0))
        gate += planar[0, :, cols]
        up += planar[1, :, cols]
        h = (gate / (1.0 + jnp.exp(-gate)) * up).astype(jnp.bfloat16)
        hidden[:, cols] = h
        narrowed += nt_dot(h, shrink_down[:, cols])
    write_hidden = pltpu.make_async_copy(hidden, hidden_out, out_sem.at[0])
    write_hidden.start()

    turned = pltpu.roll(narrowed, 64, 1)
    low = jnp.where(second_slot, turned, narrowed)[:32]
    high = jnp.where(second_slot, narrowed, turned)[32:]
    part_down[...] = jnp.where(lane_low[:32], low, high).astype(jnp.bfloat16)
    copies_c = []
    for i, off in enumerate(far_first):
        c = pltpu.make_async_remote_copy(
            src_ref=part_down,
            dst_ref=land_c.at[me],
            send_sem=send_c.at[i],
            recv_sem=recv_c,
            **peer((me + off) % n),
        )
        c.start()
        copies_c.append(c)
    land_c[me] = part_down[...]
    arrived(land_c, recv_c)
    packed = land_c[0].astype(jnp.float32)
    for i in range(1, n):
        packed += land_c[i].astype(jnp.float32)
    other = pltpu.roll(packed, 64, 1)
    reduced = jnp.concatenate(
        [jnp.where(lane_low[:32], packed, other), jnp.where(lane_low[:32], other, packed)], axis=0
    )
    reduced = jnp.where(keep, reduced, 0.0).astype(jnp.bfloat16)
    down[...] = dot(reduced, expand_down[...]).astype(jnp.bfloat16)
    write_down = pltpu.make_async_copy(down, down_out, out_sem.at[1])
    write_down.start()
    for c in copies + copies_b + copies_c:
        c.wait_send()
    write_hidden.wait()
    write_down.wait()


def per_device(
    tokens, gate_up_base, shrink_gate_up, expand_gate_up, shrink_down, expand_down, token_slot
):
    shrink_up = jnp.swapaxes(shrink_gate_up, 2, 3).reshape(256, 1024)
    down_t = jnp.swapaxes(shrink_down, 1, 2).reshape(128, 3328)
    expand_d = expand_down.reshape(128, 1024)
    slot = token_slot.reshape(1, 64)
    bf, f32 = jnp.bfloat16, jnp.float32
    dma = pltpu.SemaphoreType.DMA
    return pl.pallas_call(
        kernel,
        out_shape=(
            jax.ShapeDtypeStruct((64, 3328), bf),
            jax.ShapeDtypeStruct((64, 1024), bf),
        ),
        in_specs=[pl.BlockSpec(memory_space=pl.ANY)] * 7,
        out_specs=[pl.BlockSpec(memory_space=pl.ANY)] * 2,
        scratch_shapes=[
            pltpu.VMEM((64, 1024), bf),
            pltpu.VMEM((64, 2, 3328), bf),
            pltpu.VMEM((256, 1024), bf),
            pltpu.VMEM((2, 2, 64, 3328), bf),
            pltpu.VMEM((128, 3328), bf),
            pltpu.VMEM((128, 1024), bf),
            pltpu.VMEM((1, 64), jnp.int32),
            pltpu.VMEM((2, 64, 3328), f32),
            pltpu.VMEM((64, 3328), bf),
            pltpu.VMEM((64, 1024), bf),
            pltpu.VMEM((64, 128), f32),
            pltpu.VMEM((3, 16, 128), f32),
            pltpu.VMEM((16, 128), bf),
            pltpu.VMEM((16, 16, 128), bf),
            pltpu.VMEM((32, 128), bf),
            pltpu.VMEM((16, 32, 128), bf),
            dma((7,)),
            dma((2,)),
            dma((3,)),
            dma((3,)),
            dma((15,)),
            dma,
            dma((15,)),
            dma,
        ],
        compiler_params=pltpu.CompilerParams(
            collective_id=0, has_side_effects=True, vmem_limit_bytes=60 * 2**20
        ),
    )(tokens, gate_up_base, shrink_up, expand_gate_up, down_t, expand_d, slot)


def solution(mesh):
    placed = (
        P("dp", "tensor"),
        P("dp", None, "tensor"),
        P("dp", None, "tensor", None),
        P("dp", None, None, "tensor"),
        P("dp", "tensor", None),
        P("dp", None, "tensor"),
        P("dp"),
    )
    return jax.shard_map(
        per_device,
        mesh=mesh,
        in_specs=placed,
        out_specs=(P("dp", "tensor"), P("dp", "tensor")),
        check_vma=False,
    )
```

```python
import functools

import jax
import jax.numpy as jnp
from jax import lax
from jax.experimental import pallas as pl
from jax.experimental.pallas import tpu as pltpu
from jax.sharding import PartitionSpec as P

MESH = pl.DeviceIdType.MESH
NT = (((1,), (1,)), ((), ()))


def nt_dot(a, b):
    return lax.dot_general(a, b, NT, preferred_element_type=jnp.float32)


def dot(a, b):
    return jnp.dot(a, b, preferred_element_type=jnp.float32)


GATES = {
    3: ((1, 0),),
    4: ((0, 2),),
    7: ((2, 0), (3, 1)),
    8: ((1, 1), (0, 1)),
    11: ((3, 0),),
    12: ((2, 1), (1, 2)),
    15: ((0, 0),),
}
RELAY = 7


def kernel(
    tokens_hbm, base_hbm, shrink_up_hbm, expand_up_hbm, shrink_down_hbm, slot_hbm,
    hidden, reduced,
    tokens, base, shrink_up, expand_up, shrink_down, slot,
    planar,
    part, land_m, gate_sum, land_s, part_down, land_c,
    in_sem, send_m, recv_m, send_s, recv_s, send_c, recv_c,
):
    me = lax.axis_index("tensor")
    dp = lax.axis_index("dp")
    n = 16
    cube, spot = me // 4, me % 4

    def load(i, src, dst):
        c = pltpu.make_async_copy(src, dst, in_sem.at[i])
        c.start()
        return c

    def peer(z):
        return dict(device_id=(dp, z), device_id_type=MESH)

    def greet(z):
        pl.semaphore_signal(barrier, inc=1, **peer(z))

    barrier = pltpu.get_barrier_semaphore()
    for dst in range(4):
        @pl.when(cube == dst)
        def _():
            for gate, targets in GATES.items():
                if dst in [c for c, _ in targets]:
                    greet(gate)
    for off in (1, 2, 3):
        greet(cube * 4 + (spot + off) % 4)

    first = [load(0, tokens_hbm, tokens), load(1, shrink_up_hbm, shrink_up), load(2, slot_hbm, slot)]
    second = [load(3, base_hbm, base), load(4, expand_up_hbm, expand_up)]
    third = [load(5, shrink_down_hbm, shrink_down)]

    @pl.when(cube >= 2)
    def _():
        land_s[2] = jnp.zeros((64, 128), jnp.bfloat16)

    for c in first:
        c.wait()

    ones = jnp.sum(slot[...].astype(jnp.float32), axis=1, keepdims=True)
    row = lax.broadcasted_iota(jnp.int32, (64, 128), 0).astype(jnp.float32)
    second_slot = row >= 64.0 - ones
    lane_low = lax.broadcasted_iota(jnp.int32, (64, 128), 1) < 64
    keep = lane_low != second_slot

    both = nt_dot(tokens[...], shrink_up[...])
    cube_sum = jnp.where(second_slot, both[:, 128:], both[:, :128])
    part[...] = cube_sum.astype(jnp.bfloat16)

    greetings = 3
    for gate, targets in GATES.items():
        greetings += jnp.where(me == gate, 4 * len(targets), 0)
    pl.semaphore_wait(barrier, greetings)

    mates = []
    for off in (1, 2, 3):
        c = pltpu.make_async_remote_copy(
            src_ref=part,
            dst_ref=land_m.at[off - 1],
            send_sem=send_m.at[off - 1],
            recv_sem=recv_m.at[off - 1],
            **peer(cube * 4 + (spot + off) % 4),
        )
        c.start()
        mates.append(c)

    for c in second:
        c.wait()
    planar[0] = base[:, 0, :].astype(jnp.float32)
    planar[1] = base[:, 1, :].astype(jnp.float32)

    for i, c in enumerate(mates):
        c.wait_recv()
        cube_sum += land_m[i].astype(jnp.float32)

    def sum_arrived(i):
        pltpu.make_async_copy(land_s.at[i], land_s.at[i], recv_s.at[i]).wait()

    def gate_copies(gate):
        copies = []
        for cube_to, place in GATES[gate]:
            near_last = cube_to * 4 > gate
            for k in (3, 2, 1, 0) if near_last else (0, 1, 2, 3):
                copies.append(
                    pltpu.make_async_remote_copy(
                        src_ref=gate_sum,
                        dst_ref=land_s.at[place],
                        send_sem=send_s.at[len(copies)],
                        recv_sem=recv_s.at[place],
                        **peer(cube_to * 4 + k),
                    )
                )
        return copies

    for gate in GATES:
        @pl.when(me == gate)
        def _():
            outgoing = cube_sum
            if gate == RELAY:
                sum_arrived(0)
                outgoing += land_s[0].astype(jnp.float32)
            gate_sum[...] = outgoing.astype(jnp.bfloat16)
            for c in gate_copies(gate):
                c.start()

    for c in third:
        c.wait()

    @pl.when(me != RELAY)
    def _():
        sum_arrived(0)

    @pl.when(cube < 2)
    def _():
        sum_arrived(2)

    sum_arrived(1)
    shrunk = cube_sum
    for i in range(3):
        shrunk += land_s[i].astype(jnp.float32)
    swapped = pltpu.roll(shrunk, 64, 1)
    lhs = [
        jnp.where(keep, jnp.where(lane_low, shrunk, swapped), 0.0).astype(jnp.bfloat16),
        jnp.where(keep, jnp.where(lane_low, swapped, shrunk), 0.0).astype(jnp.bfloat16),
    ]
    narrowed = jnp.zeros((64, 128), jnp.float32)
    for k in range(13):
        cols = pl.ds(k * 256, 256)
        gate = dot(lhs[0], jnp.concatenate([expand_up[0, 0, :, cols], expand_up[1, 0, :, cols]], axis=0))
        up = dot(lhs[1], jnp.concatenate([expand_up[0, 1, :, cols], expand_up[1, 1, :, cols]], axis=0))
        gate += planar[0, :, cols]
        up += planar[1, :, cols]
        h = (gate / (1.0 + jnp.exp(-gate)) * up).astype(jnp.bfloat16)
        hidden[:, cols] = h
        narrowed += nt_dot(h, shrink_down[:, cols])

    turned = pltpu.roll(narrowed, 64, 1)
    low = jnp.where(second_slot, turned, narrowed)[:32]
    high = jnp.where(second_slot, narrowed, turned)[32:]
    part_down[...] = jnp.where(lane_low[:32], low, high).astype(jnp.bfloat16)
    copies_c = []
    for i in range(n - 1):
        c = pltpu.make_async_remote_copy(
            src_ref=part_down,
            dst_ref=land_c.at[me],
            send_sem=send_c.at[i],
            recv_sem=recv_c,
            **peer(i + jnp.where(me <= i, 1, 0)),
        )
        c.start()
        copies_c.append(c)
    land_c[me] = part_down[...]

    for c in mates:
        c.wait_send()
    for gate in GATES:
        @pl.when(me == gate)
        def _():
            for c in gate_copies(gate):
                c.wait_send()

    fifteen = land_c.at[pl.ds(0, n - 1)]
    pltpu.make_async_copy(fifteen, fifteen, recv_c).wait()
    packed = land_c[0].astype(jnp.float32)
    for i in range(1, n):
        packed += land_c[i].astype(jnp.float32)
    other = pltpu.roll(packed, 64, 1)
    spread = jnp.concatenate(
        [jnp.where(lane_low[:32], packed, other), jnp.where(lane_low[:32], other, packed)], axis=0
    )
    reduced[...] = jnp.where(keep, spread, 0.0).astype(jnp.bfloat16)
    for c in copies_c:
        c.wait_send()


def finish(hidden_in, reduced, expand_down, hidden_out, down_out, down, sem):
    rows = 16
    moves = []
    for i in range(4):
        part = pl.ds(i * rows, rows)
        c = pltpu.make_async_copy(hidden_in.at[part], hidden_out.at[part], sem.at[i])
        c.start()
        moves.append(c)
    down[...] = dot(reduced[...], expand_down[...]).astype(jnp.bfloat16)
    c = pltpu.make_async_copy(down, down_out, sem.at[4])
    c.start()
    for m in moves:
        m.wait()
    c.wait()


def per_device(
    tokens, gate_up_base, shrink_gate_up, expand_gate_up, shrink_down, expand_down, token_slot
):
    shrink_up = jnp.swapaxes(shrink_gate_up, 2, 3).reshape(256, 1024)
    down_t = jnp.swapaxes(shrink_down, 1, 2).reshape(128, 3328)
    expand_d = expand_down.reshape(128, 1024)
    slot = token_slot.reshape(1, 64)
    operands = [
        pltpu.with_memory_space_constraint(x, pltpu.HBM)
        for x in (tokens, gate_up_base, shrink_up, expand_gate_up, down_t, slot)
    ]
    bf, f32 = jnp.bfloat16, jnp.float32
    dma = pltpu.SemaphoreType.DMA
    hidden, reduced = pl.pallas_call(
        kernel,
        out_shape=(
            jax.ShapeDtypeStruct((64, 3328), bf),
            jax.ShapeDtypeStruct((64, 128), bf),
        ),
        in_specs=[pl.BlockSpec(memory_space=pltpu.HBM)] * 6,
        out_specs=[pl.BlockSpec(memory_space=pltpu.VMEM)] * 2,
        scratch_shapes=[
            pltpu.VMEM((64, 1024), bf),
            pltpu.VMEM((64, 2, 3328), bf),
            pltpu.VMEM((256, 1024), bf),
            pltpu.VMEM((2, 2, 64, 3328), bf),
            pltpu.VMEM((128, 3328), bf),
            pltpu.VMEM((1, 64), jnp.int32),
            pltpu.VMEM((2, 64, 3328), f32),
            pltpu.VMEM((64, 128), bf),
            pltpu.VMEM((3, 64, 128), bf),
            pltpu.VMEM((64, 128), bf),
            pltpu.VMEM((3, 64, 128), bf),
            pltpu.VMEM((32, 128), bf),
            pltpu.VMEM((16, 32, 128), bf),
            dma((6,)),
            dma((3,)),
            dma((3,)),
            dma((8,)),
            dma((3,)),
            dma((15,)),
            dma,
        ],
        compiler_params=pltpu.CompilerParams(
            collective_id=0, has_side_effects=True, vmem_limit_bytes=12 * 2**20
        ),
    )(*operands)
    return pl.pallas_call(
        finish,
        out_shape=(
            jax.ShapeDtypeStruct((64, 3328), bf),
            jax.ShapeDtypeStruct((64, 1024), bf),
        ),
        in_specs=[
            pl.BlockSpec(memory_space=pl.ANY),
            pl.BlockSpec(memory_space=pltpu.VMEM),
            pl.BlockSpec(memory_space=pltpu.VMEM),
        ],
        out_specs=[pl.BlockSpec(memory_space=pl.ANY)] * 2,
        scratch_shapes=[pltpu.VMEM((64, 1024), bf), dma((5,))],
        compiler_params=pltpu.CompilerParams(vmem_limit_bytes=4 * 2**20),
    )(hidden, reduced, expand_d)


def solution(mesh):
    placed = (
        P("dp", "tensor"),
        P("dp", None, "tensor"),
        P("dp", None, "tensor", None),
        P("dp", None, None, "tensor"),
        P("dp", "tensor", None),
        P("dp", None, "tensor"),
        P("dp"),
    )
    return jax.shard_map(
        per_device,
        mesh=mesh,
        in_specs=placed,
        out_specs=(P("dp", "tensor"), P("dp", "tensor")),
        check_vma=False,
    )
```

```python
import functools

import jax
import jax.numpy as jnp
from jax import lax
from jax.experimental import pallas as pl
from jax.experimental.pallas import tpu as pltpu
from jax.sharding import PartitionSpec as P

MESH = pl.DeviceIdType.MESH
NT = (((1,), (1,)), ((), ()))


def nt_dot(a, b):
    return lax.dot_general(a, b, NT, preferred_element_type=jnp.float32)


def dot(a, b):
    return jnp.dot(a, b, preferred_element_type=jnp.float32)


CUBE = [tuple(range(4 * c, 4 * c + 4)) for c in range(4)]
RELAY, FEED = 4, 3
GATES = {
    FEED: [(RELAY, 0)],
    RELAY: [(11, 0), (12, 1), (10, 0), (13, 1), (9, 0), (14, 1), (8, 0), (15, 1)] + [(z, 2) for z in (3, 2, 1, 0)],
    8: [(z, 1) for z in CUBE[1] + CUBE[0]],
    11: [(z, 0) for z in CUBE[3][::-1]],
    12: [(z, 2) for z in CUBE[1]] + [(z, 1) for z in CUBE[2]],
    15: [(z, 0) for z in CUBE[0]],
}


def kernel(
    tokens_hbm, base_hbm, shrink_up_hbm, expand_up_hbm, shrink_down_hbm, slot_hbm,
    hidden, reduced,
    tokens, base, shrink_up, expand_up, shrink_down, slot,
    planar,
    part, land_m, gate_sum, land_s, part_down, land_c,
    in_sem, send_m, recv_m, send_s, recv_s, send_c, recv_c,
):
    me = lax.axis_index("tensor")
    dp = lax.axis_index("dp")
    n = 16
    cube, spot = me // 4, me % 4

    def load(i, src, dst):
        c = pltpu.make_async_copy(src, dst, in_sem.at[i])
        c.start()
        return c

    def peer(z):
        return dict(device_id=(dp, z), device_id_type=MESH)

    def greet(z):
        pl.semaphore_signal(barrier, inc=1, **peer(z))

    barrier = pltpu.get_barrier_semaphore()
    @pl.when(cube >= 2)
    def _():
        greet(RELAY)
        greet(jnp.where(cube == 2, 12, 11))

    for off in (1, 2, 3):
        greet(cube * 4 + (spot + off) % 4)

    @pl.when(cube < 2)
    def _():
        greet(8)
        greet(jnp.where(cube == 0, 15, 12))

        @pl.when(cube == 0)
        def _():
            greet(RELAY)

        @pl.when(me == RELAY)
        def _():
            greet(FEED)

    first = [load(0, tokens_hbm, tokens), load(1, shrink_up_hbm, shrink_up), load(2, slot_hbm, slot)]
    second = [load(3, base_hbm, base), load(4, expand_up_hbm, expand_up)]
    third = [load(5, shrink_down_hbm, shrink_down)]

    for i, bare in ((0, (cube == RELAY // 4) & (me != RELAY)), (2, cube >= 2)):
        @pl.when(bare)
        def _():
            land_s[i] = jnp.zeros((64, 128), jnp.bfloat16)

    for c in first:
        c.wait()

    ones = jnp.sum(slot[...].astype(jnp.float32), axis=1, keepdims=True)
    row = lax.broadcasted_iota(jnp.int32, (64, 128), 0).astype(jnp.float32)
    second_slot = row >= 64.0 - ones
    lane_low = lax.broadcasted_iota(jnp.int32, (64, 128), 1) < 64
    keep = lane_low != second_slot

    both = nt_dot(tokens[...], shrink_up[...])
    cube_sum = jnp.where(second_slot, both[:, 128:], both[:, :128])
    own_part = cube_sum
    part[...] = cube_sum.astype(jnp.bfloat16)

    mates = [
        pltpu.make_async_remote_copy(
            src_ref=part,
            dst_ref=land_m.at[off - 1],
            send_sem=send_m.at[off - 1],
            recv_sem=recv_m.at[off - 1],
            **peer(cube * 4 + (spot + off) % 4),
        )
        for off in (1, 2, 3)
    ]

    @pl.when(me != RELAY)
    def _():
        greetings = 3
        for gate, targets in GATES.items():
            greetings += jnp.where(me == gate, len(targets), 0)
        pl.semaphore_wait(barrier, greetings)
        for c in mates:
            c.start()

    for c in second:
        c.wait()
    planar[0] = base[:, 0, :].astype(jnp.float32)
    planar[1] = base[:, 1, :].astype(jnp.float32)

    for i, c in enumerate(mates):
        c.wait_recv()
        cube_sum += land_m[i].astype(jnp.float32)

    def sum_arrived(i):
        pltpu.make_async_copy(land_s.at[i], land_s.at[i], recv_s.at[i]).wait()

    def gate_copies(gate):
        return [
            pltpu.make_async_remote_copy(
                src_ref=gate_sum.at[1 if z < gate and gate == RELAY else 0],
                dst_ref=land_s.at[place],
                send_sem=send_s.at[i],
                recv_sem=recv_s.at[place],
                **peer(z),
            )
            for i, (z, place) in enumerate(GATES[gate])
        ]

    for gate in GATES:
        @pl.when(me == gate)
        def _():
            gate_sum[0] = cube_sum.astype(jnp.bfloat16)
            if gate == RELAY:
                gate_sum[1] = cube_sum.astype(jnp.bfloat16)
                sum_arrived(0)
                fed = land_s[0].astype(jnp.float32)
                gate_sum[0] = (cube_sum + fed).astype(jnp.bfloat16)
                part[...] = (own_part + fed).astype(jnp.bfloat16)
                pl.semaphore_wait(barrier, 3 + len(GATES[gate]))
            for c in gate_copies(gate):
                c.start()
            if gate == RELAY:
                for c in mates:
                    c.start()

    for c in third:
        c.wait()

    @pl.when(cube != RELAY // 4)
    def _():
        sum_arrived(0)

    @pl.when(cube < 2)
    def _():
        sum_arrived(2)

    sum_arrived(1)
    shrunk = cube_sum
    for i in range(3):
        shrunk += land_s[i].astype(jnp.float32)
    swapped = pltpu.roll(shrunk, 64, 1)
    lhs = [
        jnp.where(keep, jnp.where(lane_low, shrunk, swapped), 0.0).astype(jnp.bfloat16),
        jnp.where(keep, jnp.where(lane_low, swapped, shrunk), 0.0).astype(jnp.bfloat16),
    ]
    for k in range(13):
        cols = pl.ds(k * 256, 256)
        gate = dot(lhs[0], jnp.concatenate([expand_up[0, 0, :, cols], expand_up[1, 0, :, cols]], axis=0))
        up = dot(lhs[1], jnp.concatenate([expand_up[0, 1, :, cols], expand_up[1, 1, :, cols]], axis=0))
        gate += planar[0, :, cols]
        up += planar[1, :, cols]
        h = (gate / (1.0 + jnp.exp(-gate)) * up).astype(jnp.bfloat16)
        hidden[:, cols] = h
    narrowed = nt_dot(hidden[...], shrink_down[...])

    turned = pltpu.roll(narrowed, 64, 1)
    low = jnp.where(second_slot, turned, narrowed)[:32]
    high = jnp.where(second_slot, narrowed, turned)[32:]
    part_down[...] = jnp.where(lane_low[:32], low, high).astype(jnp.bfloat16)
    copies_c = []
    for i in range(n - 1):
        c = pltpu.make_async_remote_copy(
            src_ref=part_down,
            dst_ref=land_c.at[me],
            send_sem=send_c.at[i],
            recv_sem=recv_c,
            **peer(i + jnp.where(me <= i, 1, 0)),
        )
        c.start()
        copies_c.append(c)
    land_c[me] = part_down[...]

    for c in mates:
        c.wait_send()
    for gate in GATES:
        @pl.when(me == gate)
        def _():
            for c in gate_copies(gate):
                c.wait_send()

    fifteen = land_c.at[pl.ds(0, n - 1)]
    pltpu.make_async_copy(fifteen, fifteen, recv_c).wait()
    packed = land_c[0].astype(jnp.float32)
    for i in range(1, n):
        packed += land_c[i].astype(jnp.float32)
    other = pltpu.roll(packed, 64, 1)
    spread = jnp.concatenate(
        [jnp.where(lane_low[:32], packed, other), jnp.where(lane_low[:32], other, packed)], axis=0
    )
    reduced[...] = jnp.where(keep, spread, 0.0).astype(jnp.bfloat16)
    for c in copies_c:
        c.wait_send()


def finish(hidden_in, reduced, expand_down, hidden_out, down_out, down, sem):
    rows = 16
    moves = []
    for i in range(4):
        part = pl.ds(i * rows, rows)
        c = pltpu.make_async_copy(hidden_in.at[part], hidden_out.at[part], sem.at[i])
        c.start()
        moves.append(c)
    down[...] = dot(reduced[...], expand_down[...]).astype(jnp.bfloat16)
    c = pltpu.make_async_copy(down, down_out, sem.at[4])
    c.start()
    for m in moves:
        m.wait()
    c.wait()


def per_device(
    tokens, gate_up_base, shrink_gate_up, expand_gate_up, shrink_down, expand_down, token_slot
):
    shrink_up = jnp.swapaxes(shrink_gate_up, 2, 3).reshape(256, 1024)
    down_t = jnp.swapaxes(shrink_down, 1, 2).reshape(128, 3328)
    expand_d = expand_down.reshape(128, 1024)
    slot = token_slot.reshape(1, 64)
    operands = [
        pltpu.with_memory_space_constraint(x, pltpu.HBM)
        for x in (tokens, gate_up_base, shrink_up, expand_gate_up, down_t, slot)
    ]
    bf, f32 = jnp.bfloat16, jnp.float32
    dma = pltpu.SemaphoreType.DMA
    hidden, reduced = pl.pallas_call(
        kernel,
        out_shape=(
            jax.ShapeDtypeStruct((64, 3328), bf),
            jax.ShapeDtypeStruct((64, 128), bf),
        ),
        in_specs=[pl.BlockSpec(memory_space=pltpu.HBM)] * 6,
        out_specs=[pl.BlockSpec(memory_space=pltpu.VMEM)] * 2,
        scratch_shapes=[
            pltpu.VMEM((64, 1024), bf),
            pltpu.VMEM((64, 2, 3328), bf),
            pltpu.VMEM((256, 1024), bf),
            pltpu.VMEM((2, 2, 64, 3328), bf),
            pltpu.VMEM((128, 3328), bf),
            pltpu.VMEM((1, 64), jnp.int32),
            pltpu.VMEM((2, 64, 3328), f32),
            pltpu.VMEM((64, 128), bf),
            pltpu.VMEM((3, 64, 128), bf),
            pltpu.VMEM((2, 64, 128), bf),
            pltpu.VMEM((3, 64, 128), bf),
            pltpu.VMEM((32, 128), bf),
            pltpu.VMEM((16, 32, 128), bf),
            dma((6,)),
            dma((3,)),
            dma((3,)),
            dma((12,)),
            dma((3,)),
            dma((15,)),
            dma,
        ],
        compiler_params=pltpu.CompilerParams(
            collective_id=0, has_side_effects=True, vmem_limit_bytes=12 * 2**20
        ),
    )(*operands)
    return pl.pallas_call(
        finish,
        out_shape=(
            jax.ShapeDtypeStruct((64, 3328), bf),
            jax.ShapeDtypeStruct((64, 1024), bf),
        ),
        in_specs=[
            pl.BlockSpec(memory_space=pl.ANY),
            pl.BlockSpec(memory_space=pltpu.VMEM),
            pl.BlockSpec(memory_space=pltpu.VMEM),
        ],
        out_specs=[pl.BlockSpec(memory_space=pl.ANY)] * 2,
        scratch_shapes=[pltpu.VMEM((64, 1024), bf), dma((5,))],
        compiler_params=pltpu.CompilerParams(vmem_limit_bytes=4 * 2**20),
    )(hidden, reduced, expand_d)


def solution(mesh):
    placed = (
        P("dp", "tensor"),
        P("dp", None, "tensor"),
        P("dp", None, "tensor", None),
        P("dp", None, None, "tensor"),
        P("dp", "tensor", None),
        P("dp", None, "tensor"),
        P("dp"),
    )
    return jax.shard_map(
        per_device,
        mesh=mesh,
        in_specs=placed,
        out_specs=(P("dp", "tensor"), P("dp", "tensor")),
        check_vma=False,
    )
```

```python
import functools

import jax
import jax.numpy as jnp
from jax import lax
from jax.experimental import pallas as pl
from jax.experimental.pallas import tpu as pltpu
from jax.sharding import PartitionSpec as P

MESH = pl.DeviceIdType.MESH
NT = (((1,), (1,)), ((), ()))


def nt_dot(a, b):
    return lax.dot_general(a, b, NT, preferred_element_type=jnp.float32)


def dot(a, b):
    return jnp.dot(a, b, preferred_element_type=jnp.float32)


CUBE = [tuple(range(4 * c, 4 * c + 4)) for c in range(4)]
RELAY, FEED = 4, 3
GATES = {
    FEED: [(RELAY, 0)],
    RELAY: [(11, 0), (12, 1), (10, 0), (13, 1), (9, 0), (14, 1), (8, 0), (15, 1)] + [(z, 2) for z in (3, 2, 1, 0)],
    8: [(z, 1) for z in CUBE[1] + CUBE[0]],
    11: [(z, 0) for z in CUBE[3][::-1]],
    12: [(z, 2) for z in CUBE[1]] + [(z, 1) for z in CUBE[2]],
    15: [(z, 0) for z in CUBE[0]],
}


def kernel(
    tokens_hbm, base_hbm, shrink_up_hbm, expand_up_hbm, shrink_down_hbm, slot_hbm,
    hidden, reduced,
    tokens, base, shrink_up, expand_up, shrink_down, slot,
    planar, shrink_down_t,
    part, land_m, gate_sum, land_s, part_down, land_c,
    in_sem, send_m, recv_m, send_s, recv_s, send_c, recv_c,
):
    me = lax.axis_index("tensor")
    dp = lax.axis_index("dp")
    n = 16
    cube, spot = me // 4, me % 4

    def load(i, src, dst):
        c = pltpu.make_async_copy(src, dst, in_sem.at[i])
        c.start()
        return c

    def peer(z):
        return dict(device_id=(dp, z), device_id_type=MESH)

    def greet(z):
        pl.semaphore_signal(barrier, inc=1, **peer(z))

    barrier = pltpu.get_barrier_semaphore()
    @pl.when(cube >= 2)
    def _():
        greet(RELAY)
        greet(jnp.where(cube == 2, 12, 11))

    for off in (1, 2, 3):
        greet(cube * 4 + (spot + off) % 4)

    @pl.when(cube < 2)
    def _():
        greet(8)
        greet(jnp.where(cube == 0, 15, 12))

        @pl.when(cube == 0)
        def _():
            greet(RELAY)

        @pl.when(me == RELAY)
        def _():
            greet(FEED)

    first = [load(0, tokens_hbm, tokens), load(1, shrink_up_hbm, shrink_up), load(2, slot_hbm, slot)]
    second = [load(3, base_hbm, base), load(4, expand_up_hbm, expand_up)]
    third = [load(5, shrink_down_hbm, shrink_down)]

    for i, bare in ((0, (cube == RELAY // 4) & (me != RELAY)), (2, cube >= 2)):
        @pl.when(bare)
        def _():
            land_s[i] = jnp.zeros((64, 128), jnp.bfloat16)

    for c in first:
        c.wait()

    ones = jnp.sum(slot[...].astype(jnp.float32), axis=1, keepdims=True)
    row = lax.broadcasted_iota(jnp.int32, (64, 128), 0).astype(jnp.float32)
    second_slot = row >= 64.0 - ones
    lane_low = lax.broadcasted_iota(jnp.int32, (64, 128), 1) < 64
    keep = lane_low != second_slot

    both = nt_dot(tokens[...], shrink_up[...])
    cube_sum = jnp.where(second_slot, both[:, 128:], both[:, :128])
    own_part = cube_sum
    part[...] = cube_sum.astype(jnp.bfloat16)

    mates = [
        pltpu.make_async_remote_copy(
            src_ref=part,
            dst_ref=land_m.at[off - 1],
            send_sem=send_m.at[off - 1],
            recv_sem=recv_m.at[off - 1],
            **peer(cube * 4 + (spot + off) % 4),
        )
        for off in (1, 2, 3)
    ]

    @pl.when(me != RELAY)
    def _():
        greetings = 3
        for gate, targets in GATES.items():
            greetings += jnp.where(me == gate, len(targets), 0)
        pl.semaphore_wait(barrier, greetings)
        for c in mates:
            c.start()

    for c in second:
        c.wait()
    planar[0] = base[:, 0, :].astype(jnp.float32)
    planar[1] = base[:, 1, :].astype(jnp.float32)

    for i, c in enumerate(mates):
        c.wait_recv()
        cube_sum += land_m[i].astype(jnp.float32)

    def sum_arrived(i):
        pltpu.make_async_copy(land_s.at[i], land_s.at[i], recv_s.at[i]).wait()

    def gate_copies(gate):
        return [
            pltpu.make_async_remote_copy(
                src_ref=gate_sum.at[1 if z < gate and gate == RELAY else 0],
                dst_ref=land_s.at[place],
                send_sem=send_s.at[i],
                recv_sem=recv_s.at[place],
                **peer(z),
            )
            for i, (z, place) in enumerate(GATES[gate])
        ]

    for gate in GATES:
        @pl.when(me == gate)
        def _():
            gate_sum[0] = cube_sum.astype(jnp.bfloat16)
            if gate == RELAY:
                gate_sum[1] = cube_sum.astype(jnp.bfloat16)
                sum_arrived(0)
                fed = land_s[0].astype(jnp.float32)
                gate_sum[0] = (cube_sum + fed).astype(jnp.bfloat16)
                part[...] = (own_part + fed).astype(jnp.bfloat16)
                pl.semaphore_wait(barrier, 3 + len(GATES[gate]))
            for c in gate_copies(gate):
                c.start()
            if gate == RELAY:
                for c in mates:
                    c.start()

    for c in third:
        c.wait()
    shrink_down_t[...] = shrink_down[...].T

    @pl.when(cube != RELAY // 4)
    def _():
        sum_arrived(0)

    @pl.when(cube < 2)
    def _():
        sum_arrived(2)

    sum_arrived(1)
    shrunk = cube_sum
    for i in range(3):
        shrunk += land_s[i].astype(jnp.float32)
    swapped = pltpu.roll(shrunk, 64, 1)
    lhs = [
        jnp.where(keep, jnp.where(lane_low, shrunk, swapped), 0.0).astype(jnp.bfloat16),
        jnp.where(keep, jnp.where(lane_low, swapped, shrunk), 0.0).astype(jnp.bfloat16),
    ]
    for k in range(13):
        cols = pl.ds(k * 256, 256)
        gate = dot(lhs[0], jnp.concatenate([expand_up[0, 0, :, cols], expand_up[1, 0, :, cols]], axis=0))
        up = dot(lhs[1], jnp.concatenate([expand_up[0, 1, :, cols], expand_up[1, 1, :, cols]], axis=0))
        gate += planar[0, :, cols]
        up += planar[1, :, cols]
        h = (gate / (1.0 + jnp.exp(-gate)) * up).astype(jnp.bfloat16)
        hidden[:, cols] = h
    narrowed = dot(hidden[...], shrink_down_t[...])

    turned = pltpu.roll(narrowed, 64, 1)
    low = jnp.where(second_slot, turned, narrowed)[:32]
    high = jnp.where(second_slot, narrowed, turned)[32:]
    part_down[...] = jnp.where(lane_low[:32], low, high).astype(jnp.bfloat16)
    copies_c = []
    for i in range(n - 1):
        c = pltpu.make_async_remote_copy(
            src_ref=part_down,
            dst_ref=land_c.at[me],
            send_sem=send_c.at[i],
            recv_sem=recv_c,
            **peer(i + jnp.where(me <= i, 1, 0)),
        )
        c.start()
        copies_c.append(c)
    land_c[me] = part_down[...]

    for c in mates:
        c.wait_send()
    for gate in GATES:
        @pl.when(me == gate)
        def _():
            for c in gate_copies(gate):
                c.wait_send()

    fifteen = land_c.at[pl.ds(0, n - 1)]
    pltpu.make_async_copy(fifteen, fifteen, recv_c).wait()
    packed = land_c[0].astype(jnp.float32)
    for i in range(1, n):
        packed += land_c[i].astype(jnp.float32)
    other = pltpu.roll(packed, 64, 1)
    spread = jnp.concatenate(
        [jnp.where(lane_low[:32], packed, other), jnp.where(lane_low[:32], other, packed)], axis=0
    )
    reduced[...] = jnp.where(keep, spread, 0.0).astype(jnp.bfloat16)
    for c in copies_c:
        c.wait_send()


def finish(hidden_in, reduced, expand_down, hidden_out, down_out, down, sem):
    rows = 16
    moves = []
    for i in range(4):
        part = pl.ds(i * rows, rows)
        c = pltpu.make_async_copy(hidden_in.at[part], hidden_out.at[part], sem.at[i])
        c.start()
        moves.append(c)
    down[...] = dot(reduced[...], expand_down[...]).astype(jnp.bfloat16)
    c = pltpu.make_async_copy(down, down_out, sem.at[4])
    c.start()
    for m in moves:
        m.wait()
    c.wait()


def per_device(
    tokens, gate_up_base, shrink_gate_up, expand_gate_up, shrink_down, expand_down, token_slot
):
    shrink_up = jnp.swapaxes(shrink_gate_up, 2, 3).reshape(256, 1024)
    down_t = jnp.swapaxes(shrink_down, 1, 2).reshape(128, 3328)
    expand_d = expand_down.reshape(128, 1024)
    slot = token_slot.reshape(1, 64)
    operands = [
        pltpu.with_memory_space_constraint(x, pltpu.HBM)
        for x in (tokens, gate_up_base, shrink_up, expand_gate_up, down_t, slot)
    ]
    bf, f32 = jnp.bfloat16, jnp.float32
    dma = pltpu.SemaphoreType.DMA
    hidden, reduced = pl.pallas_call(
        kernel,
        out_shape=(
            jax.ShapeDtypeStruct((64, 3328), bf),
            jax.ShapeDtypeStruct((64, 128), bf),
        ),
        in_specs=[pl.BlockSpec(memory_space=pltpu.HBM)] * 6,
        out_specs=[pl.BlockSpec(memory_space=pltpu.VMEM)] * 2,
        scratch_shapes=[
            pltpu.VMEM((64, 1024), bf),
            pltpu.VMEM((64, 2, 3328), bf),
            pltpu.VMEM((256, 1024), bf),
            pltpu.VMEM((2, 2, 64, 3328), bf),
            pltpu.VMEM((128, 3328), bf),
            pltpu.VMEM((1, 64), jnp.int32),
            pltpu.VMEM((2, 64, 3328), f32),
            pltpu.VMEM((3328, 128), bf),
            pltpu.VMEM((64, 128), bf),
            pltpu.VMEM((3, 64, 128), bf),
            pltpu.VMEM((2, 64, 128), bf),
            pltpu.VMEM((3, 64, 128), bf),
            pltpu.VMEM((32, 128), bf),
            pltpu.VMEM((16, 32, 128), bf),
            dma((6,)),
            dma((3,)),
            dma((3,)),
            dma((12,)),
            dma((3,)),
            dma((15,)),
            dma,
        ],
        compiler_params=pltpu.CompilerParams(
            collective_id=0, has_side_effects=True, vmem_limit_bytes=12 * 2**20
        ),
    )(*operands)
    return pl.pallas_call(
        finish,
        out_shape=(
            jax.ShapeDtypeStruct((64, 3328), bf),
            jax.ShapeDtypeStruct((64, 1024), bf),
        ),
        in_specs=[
            pl.BlockSpec(memory_space=pl.ANY),
            pl.BlockSpec(memory_space=pltpu.VMEM),
            pl.BlockSpec(memory_space=pltpu.VMEM),
        ],
        out_specs=[pl.BlockSpec(memory_space=pl.ANY)] * 2,
        scratch_shapes=[pltpu.VMEM((64, 1024), bf), dma((5,))],
        compiler_params=pltpu.CompilerParams(vmem_limit_bytes=4 * 2**20),
    )(hidden, reduced, expand_d)


def solution(mesh):
    placed = (
        P("dp", "tensor"),
        P("dp", None, "tensor"),
        P("dp", None, "tensor", None),
        P("dp", None, None, "tensor"),
        P("dp", "tensor", None),
        P("dp", None, "tensor"),
        P("dp"),
    )
    return jax.shard_map(
        per_device,
        mesh=mesh,
        in_specs=placed,
        out_specs=(P("dp", "tensor"), P("dp", "tensor")),
        check_vma=False,
    )
```

```python
import functools

import jax
import jax.numpy as jnp
from jax import lax
from jax.experimental import pallas as pl
from jax.experimental.pallas import tpu as pltpu
from jax.sharding import PartitionSpec as P

MESH = pl.DeviceIdType.MESH
NT = (((1,), (1,)), ((), ()))


def nt_dot(a, b):
    return lax.dot_general(a, b, NT, preferred_element_type=jnp.float32)


def dot(a, b):
    return jnp.dot(a, b, preferred_element_type=jnp.float32)


CUBE = [tuple(range(4 * c, 4 * c + 4)) for c in range(4)]
RELAY, FEED = 4, 3
GATES = {
    FEED: [(RELAY, 0)],
    RELAY: [(11, 0), (12, 1), (10, 0), (13, 1), (9, 0), (14, 1), (8, 0), (15, 1)] + [(z, 2) for z in (3, 2, 1, 0)],
    8: [(z, 1) for z in CUBE[1] + CUBE[0]],
    11: [(z, 0) for z in CUBE[3][::-1]],
    12: [(z, 2) for z in CUBE[1]] + [(z, 1) for z in CUBE[2]],
    15: [(z, 0) for z in CUBE[0]],
}


def kernel(
    tokens_hbm, base_hbm, shrink_up_hbm, expand_up_hbm, shrink_down_hbm, slot_hbm,
    hidden, reduced,
    tokens, base, shrink_up, expand_up, shrink_down, slot,
    planar, shrink_down_t,
    part, land_m, gate_sum, land_s, part_down, land_c,
    in_sem, send_m, recv_m, send_s, recv_s, send_c, recv_c,
):
    me = lax.axis_index("tensor")
    dp = lax.axis_index("dp")
    n = 16
    cube, spot = me // 4, me % 4

    def load(i, src, dst):
        c = pltpu.make_async_copy(src, dst, in_sem.at[i])
        c.start()
        return c

    def peer(z):
        return dict(device_id=(dp, z), device_id_type=MESH)

    def greet(z):
        pl.semaphore_signal(barrier, inc=1, **peer(z))

    barrier = pltpu.get_barrier_semaphore()
    @pl.when(cube >= 2)
    def _():
        greet(RELAY)
        greet(jnp.where(cube == 2, 12, 11))

    for off in (1, 2, 3):
        greet(cube * 4 + (spot + off) % 4)

    @pl.when(cube < 2)
    def _():
        greet(8)
        greet(jnp.where(cube == 0, 15, 12))

        @pl.when(cube == 0)
        def _():
            greet(RELAY)

        @pl.when(me == RELAY)
        def _():
            greet(FEED)

    first = [load(0, tokens_hbm, tokens), load(1, shrink_up_hbm, shrink_up), load(2, slot_hbm, slot)]
    second = [load(3, base_hbm, base), load(4, expand_up_hbm, expand_up)]
    third = [load(5, shrink_down_hbm, shrink_down)]

    for i, bare in ((0, (cube == RELAY // 4) & (me != RELAY)), (2, cube >= 2)):
        @pl.when(bare)
        def _():
            land_s[i] = jnp.zeros((64, 128), jnp.bfloat16)

    for c in first:
        c.wait()

    ones = jnp.sum(slot[...].astype(jnp.float32), axis=1, keepdims=True)
    row = lax.broadcasted_iota(jnp.int32, (64, 128), 0).astype(jnp.float32)
    second_slot = row >= 64.0 - ones
    lane_low = lax.broadcasted_iota(jnp.int32, (64, 128), 1) < 64
    keep = lane_low != second_slot

    both = nt_dot(tokens[...], shrink_up[...])
    cube_sum = jnp.where(second_slot, both[:, 128:], both[:, :128])
    own_part = cube_sum
    part[...] = cube_sum.astype(jnp.bfloat16)

    mates = []
    for k in range(3):
        up = k + jnp.where(spot <= k, 1, 0)
        down = 3 - k - jnp.where(3 - spot <= k, 1, 0)
        to = jnp.where(cube == 0, down, up)
        place = (to - spot + 4) % 4 - 1
        mates.append(
            pltpu.make_async_remote_copy(
                src_ref=part,
                dst_ref=land_m.at[place],
                send_sem=send_m.at[k],
                recv_sem=recv_m.at[place],
                **peer(cube * 4 + to),
            )
        )

    @pl.when(me != RELAY)
    def _():
        greetings = 3
        for gate, targets in GATES.items():
            greetings += jnp.where(me == gate, len(targets), 0)
        pl.semaphore_wait(barrier, greetings)
        for c in mates:
            c.start()

    for c in second:
        c.wait()
    planar[0] = base[:, 0, :].astype(jnp.float32)
    planar[1] = base[:, 1, :].astype(jnp.float32)

    for i in range(3):
        pltpu.make_async_copy(land_m.at[i], land_m.at[i], recv_m.at[i]).wait()
        cube_sum += land_m[i].astype(jnp.float32)

    def sum_arrived(i):
        pltpu.make_async_copy(land_s.at[i], land_s.at[i], recv_s.at[i]).wait()

    def gate_copies(gate):
        return [
            pltpu.make_async_remote_copy(
                src_ref=gate_sum.at[1 if z < gate and gate == RELAY else 0],
                dst_ref=land_s.at[place],
                send_sem=send_s.at[i],
                recv_sem=recv_s.at[place],
                **peer(z),
            )
            for i, (z, place) in enumerate(GATES[gate])
        ]

    for gate in GATES:
        @pl.when(me == gate)
        def _():
            gate_sum[0] = cube_sum.astype(jnp.bfloat16)
            if gate == RELAY:
                gate_sum[1] = cube_sum.astype(jnp.bfloat16)
                sum_arrived(0)
                fed = land_s[0].astype(jnp.float32)
                gate_sum[0] = (cube_sum + fed).astype(jnp.bfloat16)
                part[...] = (own_part + fed).astype(jnp.bfloat16)
                pl.semaphore_wait(barrier, 3 + len(GATES[gate]))
            for c in gate_copies(gate):
                c.start()
            if gate == RELAY:
                for c in mates:
                    c.start()

    for c in third:
        c.wait()
    shrink_down_t[...] = shrink_down[...].T

    @pl.when(cube != RELAY // 4)
    def _():
        sum_arrived(0)

    @pl.when(cube < 2)
    def _():
        sum_arrived(2)

    sum_arrived(1)
    shrunk = cube_sum
    for i in range(3):
        shrunk += land_s[i].astype(jnp.float32)
    swapped = pltpu.roll(shrunk, 64, 1)
    lhs = [
        jnp.where(keep, jnp.where(lane_low, shrunk, swapped), 0.0).astype(jnp.bfloat16),
        jnp.where(keep, jnp.where(lane_low, swapped, shrunk), 0.0).astype(jnp.bfloat16),
    ]
    for k in range(13):
        cols = pl.ds(k * 256, 256)
        gate = dot(lhs[0], jnp.concatenate([expand_up[0, 0, :, cols], expand_up[1, 0, :, cols]], axis=0))
        up = dot(lhs[1], jnp.concatenate([expand_up[0, 1, :, cols], expand_up[1, 1, :, cols]], axis=0))
        gate += planar[0, :, cols]
        up += planar[1, :, cols]
        h = (gate / (1.0 + jnp.exp(-gate)) * up).astype(jnp.bfloat16)
        hidden[:, cols] = h
    narrowed = dot(hidden[...], shrink_down_t[...])

    turned = pltpu.roll(narrowed, 64, 1)
    low = jnp.where(second_slot, turned, narrowed)[:32]
    high = jnp.where(second_slot, narrowed, turned)[32:]
    part_down[...] = jnp.where(lane_low[:32], low, high).astype(jnp.bfloat16)
    copies_c = []
    for i in range(n - 1):
        c = pltpu.make_async_remote_copy(
            src_ref=part_down,
            dst_ref=land_c.at[me],
            send_sem=send_c.at[i],
            recv_sem=recv_c,
            **peer(i + jnp.where(me <= i, 1, 0)),
        )
        c.start()
        copies_c.append(c)
    land_c[me] = part_down[...]

    for c in mates:
        c.wait_send()
    for gate in GATES:
        @pl.when(me == gate)
        def _():
            for c in gate_copies(gate):
                c.wait_send()

    fifteen = land_c.at[pl.ds(0, n - 1)]
    pltpu.make_async_copy(fifteen, fifteen, recv_c).wait()
    packed = land_c[0].astype(jnp.float32)
    for i in range(1, n):
        packed += land_c[i].astype(jnp.float32)
    other = pltpu.roll(packed, 64, 1)
    spread = jnp.concatenate(
        [jnp.where(lane_low[:32], packed, other), jnp.where(lane_low[:32], other, packed)], axis=0
    )
    reduced[...] = jnp.where(keep, spread, 0.0).astype(jnp.bfloat16)
    for c in copies_c:
        c.wait_send()


def finish(hidden_in, reduced, expand_down, hidden_out, down_out, down, sem):
    rows = 16
    moves = []
    for i in range(4):
        part = pl.ds(i * rows, rows)
        c = pltpu.make_async_copy(hidden_in.at[part], hidden_out.at[part], sem.at[i])
        c.start()
        moves.append(c)
    down[...] = dot(reduced[...], expand_down[...]).astype(jnp.bfloat16)
    c = pltpu.make_async_copy(down, down_out, sem.at[4])
    c.start()
    for m in moves:
        m.wait()
    c.wait()


def per_device(
    tokens, gate_up_base, shrink_gate_up, expand_gate_up, shrink_down, expand_down, token_slot
):
    shrink_up = jnp.swapaxes(shrink_gate_up, 2, 3).reshape(256, 1024)
    down_t = jnp.swapaxes(shrink_down, 1, 2).reshape(128, 3328)
    expand_d = expand_down.reshape(128, 1024)
    slot = token_slot.reshape(1, 64)
    operands = [
        pltpu.with_memory_space_constraint(x, pltpu.HBM)
        for x in (tokens, gate_up_base, shrink_up, expand_gate_up, down_t, slot)
    ]
    bf, f32 = jnp.bfloat16, jnp.float32
    dma = pltpu.SemaphoreType.DMA
    hidden, reduced = pl.pallas_call(
        kernel,
        out_shape=(
            jax.ShapeDtypeStruct((64, 3328), bf),
            jax.ShapeDtypeStruct((64, 128), bf),
        ),
        in_specs=[pl.BlockSpec(memory_space=pltpu.HBM)] * 6,
        out_specs=[pl.BlockSpec(memory_space=pltpu.VMEM)] * 2,
        scratch_shapes=[
            pltpu.VMEM((64, 1024), bf),
            pltpu.VMEM((64, 2, 3328), bf),
            pltpu.VMEM((256, 1024), bf),
            pltpu.VMEM((2, 2, 64, 3328), bf),
            pltpu.VMEM((128, 3328), bf),
            pltpu.VMEM((1, 64), jnp.int32),
            pltpu.VMEM((2, 64, 3328), f32),
            pltpu.VMEM((3328, 128), bf),
            pltpu.VMEM((64, 128), bf),
            pltpu.VMEM((3, 64, 128), bf),
            pltpu.VMEM((2, 64, 128), bf),
            pltpu.VMEM((3, 64, 128), bf),
            pltpu.VMEM((32, 128), bf),
            pltpu.VMEM((16, 32, 128), bf),
            dma((6,)),
            dma((3,)),
            dma((3,)),
            dma((12,)),
            dma((3,)),
            dma((15,)),
            dma,
        ],
        compiler_params=pltpu.CompilerParams(
            collective_id=0, has_side_effects=True, vmem_limit_bytes=12 * 2**20
        ),
    )(*operands)
    return pl.pallas_call(
        finish,
        out_shape=(
            jax.ShapeDtypeStruct((64, 3328), bf),
            jax.ShapeDtypeStruct((64, 1024), bf),
        ),
        in_specs=[
            pl.BlockSpec(memory_space=pl.ANY),
            pl.BlockSpec(memory_space=pltpu.VMEM),
            pl.BlockSpec(memory_space=pltpu.VMEM),
        ],
        out_specs=[pl.BlockSpec(memory_space=pl.ANY)] * 2,
        scratch_shapes=[pltpu.VMEM((64, 1024), bf), dma((5,))],
        compiler_params=pltpu.CompilerParams(vmem_limit_bytes=4 * 2**20),
    )(hidden, reduced, expand_d)


def solution(mesh):
    placed = (
        P("dp", "tensor"),
        P("dp", None, "tensor"),
        P("dp", None, "tensor", None),
        P("dp", None, None, "tensor"),
        P("dp", "tensor", None),
        P("dp", None, "tensor"),
        P("dp"),
    )
    return jax.shard_map(
        per_device,
        mesh=mesh,
        in_specs=placed,
        out_specs=(P("dp", "tensor"), P("dp", "tensor")),
        check_vma=False,
    )
```

```python
import functools

import jax
import jax.numpy as jnp
from jax import lax
from jax.experimental import pallas as pl
from jax.experimental.pallas import tpu as pltpu
from jax.sharding import PartitionSpec as P

MESH = pl.DeviceIdType.MESH
NT = (((1,), (1,)), ((), ()))


def nt_dot(a, b):
    return lax.dot_general(a, b, NT, preferred_element_type=jnp.float32)


def dot(a, b):
    return jnp.dot(a, b, preferred_element_type=jnp.float32)


CUBE = [tuple(range(4 * c, 4 * c + 4)) for c in range(4)]
RELAY, FEED = 4, 3
GATES = {
    FEED: [(RELAY, 0)],
    RELAY: [(11, 0), (12, 1), (10, 0), (13, 1), (9, 0), (14, 1), (8, 0), (15, 1)] + [(z, 2) for z in (3, 2, 1, 0)],
    8: [(z, 1) for z in CUBE[1] + CUBE[0]],
    11: [(z, 0) for z in CUBE[3][::-1]],
    12: [(z, 2) for z in CUBE[1]] + [(z, 1) for z in CUBE[2]],
    15: [(z, 0) for z in CUBE[0]],
}


def kernel(
    tokens_hbm, base_hbm, shrink_up_hbm, expand_up_hbm, shrink_down_hbm, slot_hbm,
    hidden, reduced,
    tokens, base, shrink_up, expand_up, shrink_down, slot,
    planar, shrink_down_t,
    part, land_m, gate_sum, land_s, part_down, land_c,
    in_sem, send_m, recv_m, send_s, recv_s, send_c, recv_c,
):
    me = lax.axis_index("tensor")
    dp = lax.axis_index("dp")
    n = 16
    cube, spot = me // 4, me % 4

    def load(i, src, dst):
        c = pltpu.make_async_copy(src, dst, in_sem.at[i])
        c.start()
        return c

    def peer(z):
        return dict(device_id=(dp, z), device_id_type=MESH)

    def greet(z):
        pl.semaphore_signal(barrier, inc=1, **peer(z))

    barrier = pltpu.get_barrier_semaphore()
    @pl.when(cube >= 2)
    def _():
        greet(RELAY)
        greet(jnp.where(cube == 2, 12, 11))

    first = [load(0, tokens_hbm, tokens), load(1, shrink_up_hbm, shrink_up), load(2, slot_hbm, slot)]

    for off in (1, 2, 3):
        greet(cube * 4 + (spot + off) % 4)

    @pl.when(cube < 2)
    def _():
        greet(8)
        greet(jnp.where(cube == 0, 15, 12))

        @pl.when(cube == 0)
        def _():
            greet(RELAY)

        @pl.when(me == RELAY)
        def _():
            greet(FEED)

    second = [load(3, base_hbm, base), load(4, expand_up_hbm, expand_up)]
    third = [load(5, shrink_down_hbm, shrink_down)]

    for i, bare in ((0, (cube == RELAY // 4) & (me != RELAY)), (2, cube >= 2)):
        @pl.when(bare)
        def _():
            land_s[i] = jnp.zeros((64, 128), jnp.bfloat16)

    for c in first:
        c.wait()

    ones = jnp.sum(slot[...].astype(jnp.float32), axis=1, keepdims=True)
    row = lax.broadcasted_iota(jnp.int32, (64, 128), 0).astype(jnp.float32)
    second_slot = row >= 64.0 - ones
    lane_low = lax.broadcasted_iota(jnp.int32, (64, 128), 1) < 64
    keep = lane_low != second_slot

    both = nt_dot(tokens[...], shrink_up[...])
    cube_sum = jnp.where(second_slot, both[:, 128:], both[:, :128])
    own_part = cube_sum
    part[...] = cube_sum.astype(jnp.bfloat16)

    mates = []
    for k in range(3):
        up = k + jnp.where(spot <= k, 1, 0)
        down = 3 - k - jnp.where(3 - spot <= k, 1, 0)
        to = jnp.where(cube == 0, down, up)
        place = (to - spot + 4) % 4 - 1
        mates.append(
            pltpu.make_async_remote_copy(
                src_ref=part,
                dst_ref=land_m.at[place],
                send_sem=send_m.at[k],
                recv_sem=recv_m.at[place],
                **peer(cube * 4 + to),
            )
        )

    @pl.when(me != RELAY)
    def _():
        greetings = 3
        for gate, targets in GATES.items():
            greetings += jnp.where(me == gate, len(targets), 0)
        pl.semaphore_wait(barrier, greetings)
        for c in mates:
            c.start()

    for c in second:
        c.wait()
    planar[0] = base[:, 0, :].astype(jnp.float32)
    planar[1] = base[:, 1, :].astype(jnp.float32)

    for i in range(3):
        pltpu.make_async_copy(land_m.at[i], land_m.at[i], recv_m.at[i]).wait()
        cube_sum += land_m[i].astype(jnp.float32)

    def sum_arrived(i):
        pltpu.make_async_copy(land_s.at[i], land_s.at[i], recv_s.at[i]).wait()

    def gate_copies(gate):
        return [
            pltpu.make_async_remote_copy(
                src_ref=gate_sum.at[1 if z < gate and gate == RELAY else 0],
                dst_ref=land_s.at[place],
                send_sem=send_s.at[i],
                recv_sem=recv_s.at[place],
                **peer(z),
            )
            for i, (z, place) in enumerate(GATES[gate])
        ]

    for gate in GATES:
        @pl.when(me == gate)
        def _():
            gate_sum[0] = cube_sum.astype(jnp.bfloat16)
            if gate == RELAY:
                gate_sum[1] = cube_sum.astype(jnp.bfloat16)
                sum_arrived(0)
                fed = land_s[0].astype(jnp.float32)
                gate_sum[0] = (cube_sum + fed).astype(jnp.bfloat16)
                part[...] = (own_part + fed).astype(jnp.bfloat16)
                pl.semaphore_wait(barrier, 3 + len(GATES[gate]))
            for c in gate_copies(gate):
                c.start()
            if gate == RELAY:
                for c in mates:
                    c.start()

    for c in third:
        c.wait()
    shrink_down_t[...] = shrink_down[...].T

    @pl.when(cube != RELAY // 4)
    def _():
        sum_arrived(0)

    @pl.when(cube < 2)
    def _():
        sum_arrived(2)

    sum_arrived(1)
    shrunk = cube_sum
    for i in range(3):
        shrunk += land_s[i].astype(jnp.float32)
    swapped = pltpu.roll(shrunk, 64, 1)
    lhs = [
        jnp.where(keep, jnp.where(lane_low, shrunk, swapped), 0.0).astype(jnp.bfloat16),
        jnp.where(keep, jnp.where(lane_low, swapped, shrunk), 0.0).astype(jnp.bfloat16),
    ]
    for k in range(13):
        cols = pl.ds(k * 256, 256)
        gate = dot(lhs[0], jnp.concatenate([expand_up[0, 0, :, cols], expand_up[1, 0, :, cols]], axis=0))
        up = dot(lhs[1], jnp.concatenate([expand_up[0, 1, :, cols], expand_up[1, 1, :, cols]], axis=0))
        gate += planar[0, :, cols]
        up += planar[1, :, cols]
        h = (gate / (1.0 + jnp.exp(-gate)) * up).astype(jnp.bfloat16)
        hidden[:, cols] = h
    narrowed = dot(hidden[...], shrink_down_t[...])

    turned = pltpu.roll(narrowed, 64, 1)
    low = jnp.where(second_slot, turned, narrowed)[:32]
    high = jnp.where(second_slot, narrowed, turned)[32:]
    part_down[...] = jnp.where(lane_low[:32], low, high).astype(jnp.bfloat16)
    copies_c = []
    for i in range(n - 1):
        c = pltpu.make_async_remote_copy(
            src_ref=part_down,
            dst_ref=land_c.at[me],
            send_sem=send_c.at[i],
            recv_sem=recv_c,
            **peer(i + jnp.where(me <= i, 1, 0)),
        )
        c.start()
        copies_c.append(c)
    land_c[me] = part_down[...]

    for c in mates:
        c.wait_send()
    for gate in GATES:
        @pl.when(me == gate)
        def _():
            for c in gate_copies(gate):
                c.wait_send()

    fifteen = land_c.at[pl.ds(0, n - 1)]
    pltpu.make_async_copy(fifteen, fifteen, recv_c).wait()
    packed = land_c[0].astype(jnp.float32)
    for i in range(1, n):
        packed += land_c[i].astype(jnp.float32)
    other = pltpu.roll(packed, 64, 1)
    spread = jnp.concatenate(
        [jnp.where(lane_low[:32], packed, other), jnp.where(lane_low[:32], other, packed)], axis=0
    )
    reduced[...] = jnp.where(keep, spread, 0.0).astype(jnp.bfloat16)
    for c in copies_c:
        c.wait_send()


def finish(hidden_in, reduced, expand_down, hidden_out, down_out, down, sem):
    rows = 16
    moves = []
    for i in range(4):
        part = pl.ds(i * rows, rows)
        c = pltpu.make_async_copy(hidden_in.at[part], hidden_out.at[part], sem.at[i])
        c.start()
        moves.append(c)
    down[...] = dot(reduced[...], expand_down[...]).astype(jnp.bfloat16)
    c = pltpu.make_async_copy(down, down_out, sem.at[4])
    c.start()
    for m in moves:
        m.wait()
    c.wait()


def per_device(
    tokens, gate_up_base, shrink_gate_up, expand_gate_up, shrink_down, expand_down, token_slot
):
    shrink_up = jnp.swapaxes(shrink_gate_up, 2, 3).reshape(256, 1024)
    down_t = jnp.swapaxes(shrink_down, 1, 2).reshape(128, 3328)
    expand_d = expand_down.reshape(128, 1024)
    slot = token_slot.reshape(1, 64)
    operands = [
        pltpu.with_memory_space_constraint(x, pltpu.HBM)
        for x in (tokens, gate_up_base, shrink_up, expand_gate_up, down_t, slot)
    ]
    bf, f32 = jnp.bfloat16, jnp.float32
    dma = pltpu.SemaphoreType.DMA
    hidden, reduced = pl.pallas_call(
        kernel,
        out_shape=(
            jax.ShapeDtypeStruct((64, 3328), bf),
            jax.ShapeDtypeStruct((64, 128), bf),
        ),
        in_specs=[pl.BlockSpec(memory_space=pltpu.HBM)] * 6,
        out_specs=[pl.BlockSpec(memory_space=pltpu.VMEM)] * 2,
        scratch_shapes=[
            pltpu.VMEM((64, 1024), bf),
            pltpu.VMEM((64, 2, 3328), bf),
            pltpu.VMEM((256, 1024), bf),
            pltpu.VMEM((2, 2, 64, 3328), bf),
            pltpu.VMEM((128, 3328), bf),
            pltpu.VMEM((1, 64), jnp.int32),
            pltpu.VMEM((2, 64, 3328), f32),
            pltpu.VMEM((3328, 128), bf),
            pltpu.VMEM((64, 128), bf),
            pltpu.VMEM((3, 64, 128), bf),
            pltpu.VMEM((2, 64, 128), bf),
            pltpu.VMEM((3, 64, 128), bf),
            pltpu.VMEM((32, 128), bf),
            pltpu.VMEM((16, 32, 128), bf),
            dma((6,)),
            dma((3,)),
            dma((3,)),
            dma((12,)),
            dma((3,)),
            dma((15,)),
            dma,
        ],
        compiler_params=pltpu.CompilerParams(
            collective_id=0, has_side_effects=True, vmem_limit_bytes=12 * 2**20
        ),
    )(*operands)
    return pl.pallas_call(
        finish,
        out_shape=(
            jax.ShapeDtypeStruct((64, 3328), bf),
            jax.ShapeDtypeStruct((64, 1024), bf),
        ),
        in_specs=[
            pl.BlockSpec(memory_space=pl.ANY),
            pl.BlockSpec(memory_space=pltpu.VMEM),
            pl.BlockSpec(memory_space=pltpu.VMEM),
        ],
        out_specs=[pl.BlockSpec(memory_space=pl.ANY)] * 2,
        scratch_shapes=[pltpu.VMEM((64, 1024), bf), dma((5,))],
        compiler_params=pltpu.CompilerParams(vmem_limit_bytes=4 * 2**20),
    )(hidden, reduced, expand_d)


def solution(mesh):
    placed = (
        P("dp", "tensor"),
        P("dp", None, "tensor"),
        P("dp", None, "tensor", None),
        P("dp", None, None, "tensor"),
        P("dp", "tensor", None),
        P("dp", None, "tensor"),
        P("dp"),
    )
    return jax.shard_map(
        per_device,
        mesh=mesh,
        in_specs=placed,
        out_specs=(P("dp", "tensor"), P("dp", "tensor")),
        check_vma=False,
    )
```
